128 devices in a mesh: replica: 64 (over z, y, x), shard: 2 (over core).
Axes of the slice: x: 4, y: 4, z: 4, core: 2. Of those that a mesh axis runs over, the one named last changes fastest.
Arguments:
- hidden_rows: bfloat16 [32768, 6144], P(('replica', 'shard')), may hold values from -6 to 6
- row_counts: int32 [128], P(('replica', 'shard')), may hold values from 1 to 256, 16384 in all
- target_rows: bfloat16 [32768, 2048], P(('replica', 'shard')), may hold values from -6 to 6
- joined_weight: bfloat16 [6144, 2048], P(('replica', 'shard')), may hold values from -0.078125 to 0.078125
- norm_gain: float32 [2048], replicated, may hold values from 0.1 to 1.9
Outputs:
- weight_step: bfloat16 [6144, 2048], P(('replica', 'shard'))
The draws below stay inside these ranges and needn't reach their ends.
Inputs may be any that keep to these rules, and one draw needn't show every extreme that they name: Device p's live rows are its first row_counts[p] slots; the counts sum to 16384, and some device has all 256 slots live.
All inputs are finite; a program needn't handle non-finite values.
Results may differ from the reference program's by a relative error of at most 0.009.
Values may be sent and summed in bfloat16 or wider, within the bound.
No kernel may reach another device: no remote copies, remote signals or barrier semaphores. Data moves between devices by JAX's collectives and lax.ppermute only.
A program may use at most 128 MiB of HBM per device.

```python
import math
import jax
import jax.numpy as jnp
import numpy as np
from jax import lax

D = 2048
DW = 2048
MEAN = 128
PROD = 256
SOURCES = 128
SLOTS = 32768
BLOCK = 48
N_REPLICA = 64
N_SHARD = 2


def level_of(rng, dims, pieces, least, largest):
    level = 1.0
    for dim, blocks in pieces:
        steps = jax.random.uniform(jax.random.fold_in(jax.random.fold_in(rng, 6), dim), (blocks,), jnp.float32, least / len(pieces), largest / len(pieces))
        level = level * jnp.repeat(jnp.exp(steps), dims[dim] // blocks).reshape((-1,) + (1,) * (len(dims) - 1 - dim))
    return level


def length_profile(number_of, total, limit, lean):
    loads = [(1 << 20) // math.isqrt(standing ** lean) + 1 for standing in range(2, number_of + 1)]
    spare, holding = total - limit - (number_of - 1), [1] * (number_of - 1)
    while spare > 0:
        candidates = [i for i in range(number_of - 1) if holding[i] < limit]
        mass, budget = sum([loads[i] for i in candidates]), spare
        for i in candidates:
            more = min(limit - holding[i], max(1, budget * loads[i] // mass), spare)
            holding[i] = holding[i] + more
            spare = spare - more
    return np.array([limit] + holding)


def uneven_parts(own_key, count, total, bound, skew):
    if count == 2:
        one = jax.random.randint(own_key, (), max(1, total - bound), min(bound, total - 1) + 1)
        return jnp.stack([one, total - one])
    tallies = jnp.asarray(length_profile(count, total, bound, skew), jnp.int32)
    twos = (count - 1) // 2
    source_of, receiver = tallies[1:1 + 2 * twos:2], tallies[2:2 + 2 * twos:2]
    margin = jnp.minimum(source_of - 1, bound - receiver)
    passed = jax.random.randint(jax.random.fold_in(own_key, 1), (twos,), 0, 1 << 20) % (margin + 1)
    tallies = tallies.at[1:1 + 2 * twos:2].set(source_of - passed).at[2:2 + 2 * twos:2].set(receiver + passed)
    return tallies[jax.random.permutation(jax.random.fold_in(own_key, 2), count)]


def centred(stream_key, shape, width, reach, cuts=(), kind=jnp.bfloat16):
    result = width * jax.random.normal(stream_key, shape, jnp.float32)
    if cuts:
        result = result * level_of(stream_key, shape, cuts, -0.22, 0.18)
    return jnp.clip(result, -reach, reach).astype(kind)


def setup_inputs(seed: int = 0) -> dict:
    key_list = jax.random.split(jax.random.key(seed), 6)
    hidden_rows = centred(key_list[0], (SLOTS, 3 * D), 1.0, 6.0, ((0, 128),))
    row_counts = uneven_parts(key_list[1], SOURCES, MEAN * SOURCES, PROD, 2).astype(jnp.int32)
    target_rows = centred(key_list[2], (SLOTS, DW), 1.0, 6.0, ((0, 128),))
    joined_weight = centred(key_list[3], (3 * D, DW), (3 * D) ** -0.5, 0.078125, ((0, 128),))
    norm_gain = jnp.clip(1.0 + 0.18 * jax.random.normal(key_list[4], (DW,), jnp.float32), 0.1, 1.9)
    return {"hidden_rows": hidden_rows, "row_counts": row_counts, "target_rows": target_rows, "joined_weight": joined_weight, "norm_gain": norm_gain}


epsilon = 1e-06

def normalize_rows(values):
    return -values * lax.rsqrt(lax.optimization_barrier(jnp.mean(values * values, axis=-1, keepdims=True)) + epsilon)

def reference(hidden_rows, row_counts, target_rows, joined_weight, norm_gain):
    slot_index = jnp.arange(PROD, dtype=jnp.int32)
    live = (slot_index[None, :] < row_counts[:, None]).astype(jnp.float32).reshape(-1, 1)
    blocks = hidden_rows.reshape(SLOTS, N_REPLICA, N_SHARD, BLOCK)
    weights = joined_weight.reshape(N_REPLICA, N_SHARD, BLOCK, DW)
    joined = jnp.zeros((hidden_rows.shape[0], DW), jnp.float32)
    for set_index in range(N_SHARD):
        inputs = blocks[:, :, set_index, :].reshape(SLOTS, N_REPLICA * BLOCK)
        matrix = weights[:, set_index].reshape(N_REPLICA * BLOCK, DW)
        product = jnp.dot(inputs, matrix, preferred_element_type=jnp.float32)
        rounded = lax.optimization_barrier(product.astype(jnp.bfloat16))
        joined = joined + rounded.astype(jnp.float32)
    inverse = lax.rsqrt(lax.optimization_barrier(jnp.mean(joined * joined, axis=1, keepdims=True)) + epsilon)
    normed = joined * inverse
    error = live * (normed * norm_gain - target_rows.astype(jnp.float32))
    scaled = error * norm_gain
    joined_grad = (inverse * (scaled - normed * lax.optimization_barrier(jnp.mean(scaled * normed, axis=1, keepdims=True)))).astype(jnp.bfloat16)
    weight_grad = lax.dot_general(hidden_rows, joined_grad, (((0,), (0,)), ((), ())), preferred_element_type=jnp.float32)
    weight_step = normalize_rows(weight_grad).astype(jnp.bfloat16)
    return weight_step
```

```python
import jax
import jax.numpy as jnp
from jax import lax
from jax.experimental import pallas as pl
from jax.experimental.pallas import tpu as pltpu
from jax.sharding import PartitionSpec as P

epsilon = 1e-06
AXES = ("replica", "shard")
STRIDE = {"z": 16, "y": 4, "x": 1}
ROUNDS = (("z", "y", "x"), ("x", "z", "y"), ("y", "x", "z"))
F32, BF16 = jnp.float32, jnp.bfloat16


def half_place(a, core):
    if core == 0:
        return a // 2, a % 2
    return (a + 1) // 2 % 2, a // 2


def chips():
    return [(z, y, x) for z in range(4) for y in range(4) for x in range(4)]


def device(z, y, x, core):
    return (z * 16 + y * 4 + x) * 2 + core


def cubes():
    groups = {}
    for z, y, x in chips():
        for core in range(2):
            halves, places = zip(*(half_place(a, core) for a in (z, y, x)))
            groups.setdefault((core, halves), {})[places] = device(z, y, x, core)
    return [[members[k] for k in sorted(members)] for members in groups.values()]


def swap_pairs(axis):
    pairs = []
    for r in range(64):
        for core in range(2):
            a = r // STRIDE[axis] % 4
            other = r + ((a ^ (3 if core == 0 else 1)) - a) * STRIDE[axis]
            pairs.append((r * 2 + core, other * 2 + core))
    return pairs


def swap(value, axis):
    return lax.ppermute(value, AXES, swap_pairs(axis))


def swap_core(value):
    return lax.ppermute(value, "shard", [(0, 1), (1, 0)])


def cube_exchange(value):
    return lax.all_to_all(value, AXES, 0, 0, axis_index_groups=cubes(), tiled=True)


def arrange_kernel(rows_ref, out_ref):
    step = pl.program_id(0)
    z, y = step // 4, step % 4
    replica, core = lax.axis_index("replica"), lax.axis_index("shard")
    mine = {"z": replica // 16, "y": replica // 4 % 4, "x": replica % 4}
    turned = rows_ref[...].T
    for x in range(4):
        for owner in range(2):
            at = {"z": z, "y": y, "x": x}
            flip, place = {}, {}
            for axis in "zyx":
                half, place[axis] = half_place(at[axis], owner)
                own_half, _ = half_place(mine[axis], owner)
                flip[axis] = lax.rem(half + own_half, 2)
            slot = place["z"] * 4 + place["y"] * 2 + place["x"]
            away = lax.rem(core + owner, 2)
            for s, order in enumerate(ROUNDS):
                chunk = flip[order[0]] + 2 * flip[order[1]] + 4 * flip[order[2]]
                first = ((x * 2 + owner) * 3 + s) * 16
                out_ref[away, s, chunk, slot] = turned[first : first + 16]


def arrange(hidden_rows):
    rows = hidden_rows.shape[0]
    return pl.pallas_call(
        arrange_kernel,
        grid=(16,),
        in_specs=[pl.BlockSpec((rows, 384), lambda i: (0, i))],
        out_specs=pl.BlockSpec((2, 3, 8, 8, 16, rows), lambda i: (0,) * 6),
        out_shape=jax.ShapeDtypeStruct((2, 3, 8, 8, 16, rows), BF16),
        compiler_params=pltpu.CompilerParams(vmem_limit_bytes=32 << 20),
        cost_estimate=pl.CostEstimate(flops=0, bytes_accessed=4 * rows * 6144, transcendentals=0),
    )(hidden_rows)


def forward_kernel(n, started, finished, *refs):
    rows_ref, pieces = refs[0], refs[1 : n + 1]
    out_ref = refs[-1]
    total = refs[n + 1][...] if started is not None else None
    for i, piece in enumerate(pieces):
        q, s = finished[i]
        part = jnp.dot(rows_ref[s, :, q * 256 : (q + 1) * 256], piece[...], preferred_element_type=F32)
        total = part if total is None else total + part
    out_ref[...] = total.astype(out_ref.dtype)


def forward(rows, pieces, places, total, dtype):
    m, width, cols = rows.shape[1], pieces[0].shape[1], 512
    n = len(pieces)

    def kernel(*refs):
        forward_kernel(n, total, places, *refs)

    operands = [rows, *pieces] + ([total] if total is not None else [])
    return pl.pallas_call(
        kernel,
        grid=(width // cols,),
        in_specs=[pl.BlockSpec(rows.shape, lambda j: (0, 0, 0))]
        + [pl.BlockSpec((256, cols), lambda j: (0, j))] * n
        + [pl.BlockSpec((m, cols), lambda j: (0, j))] * (total is not None),
        out_specs=pl.BlockSpec((m, cols), lambda j: (0, j)),
        out_shape=jax.ShapeDtypeStruct((m, width), dtype),
        compiler_params=pltpu.CompilerParams(vmem_limit_bytes=40 << 20),
        cost_estimate=pl.CostEstimate(flops=2 * m * 256 * n * width, bytes_accessed=n * 512 * width + 6 * m * width, transcendentals=0),
    )(*operands)


def grad_kernel(count_ref, own_ref, other_ref, target_ref, gain_ref, out_ref):
    tile = out_ref.shape[0]
    row = lax.broadcasted_iota(jnp.int32, (tile, 1), 0) + pl.program_id(0) * tile
    live = (row < count_ref[0]).astype(F32)
    joined = own_ref[...].astype(F32) + other_ref[...].astype(F32)
    gain = gain_ref[...]
    inverse = lax.rsqrt(jnp.mean(joined * joined, axis=1, keepdims=True) + epsilon)
    normed = joined * inverse
    error = live * (normed * gain - target_ref[...].astype(F32))
    scaled = error * gain
    mean = jnp.mean(scaled * normed, axis=1, keepdims=True)
    out_ref[...] = (inverse * (scaled - normed * mean)).astype(BF16)


def joined_grad_of(row_counts, own, other, target_rows, norm_gain):
    rows, width = target_rows.shape
    tile = 64
    block = pl.BlockSpec((tile, width), lambda i: (i, 0))
    return pl.pallas_call(
        grad_kernel,
        grid=(rows // tile,),
        in_specs=[pl.BlockSpec(memory_space=pltpu.SMEM), block, block, block, pl.BlockSpec((1, width), lambda i: (0, 0))],
        out_specs=block,
        out_shape=jax.ShapeDtypeStruct((rows, width), BF16),
        compiler_params=pltpu.CompilerParams(vmem_limit_bytes=32 << 20),
        cost_estimate=pl.CostEstimate(flops=12 * rows * width, bytes_accessed=8 * rows * width, transcendentals=rows),
    )(row_counts, own, other, target_rows, norm_gain.reshape(1, width))


def normalize_rows(values):
    return -values * lax.rsqrt(jnp.mean(values * values, axis=-1, keepdims=True) + epsilon)


def local(hidden_rows, row_counts, target_rows, joined_weight, norm_gain):
    row_total, width = target_rows.shape
    streams = range(3)

    near = cube_exchange(jnp.tile(joined_weight, (8, 1))).reshape(8, 3, 16, width)
    first = [near[:, s].reshape(128, width) for s in streams]
    second = [swap(first[s], ROUNDS[s][0]) for s in streams]
    quarter = [[jnp.concatenate([first[s], second[s]], 0) for s in streams]]
    quarter.append([swap(quarter[0][s], ROUNDS[s][1]) for s in streams])
    quarter.append([swap(quarter[0][s], ROUNDS[s][2]) for s in streams])
    quarter.append([swap(quarter[1][s], ROUNDS[s][2]) for s in streams])

    both = arrange(hidden_rows).reshape(2, 3, 1024, row_total)
    features = jnp.concatenate([both[0], swap_core(both[1])], axis=-1)
    rows = jnp.swapaxes(features, 1, 2)

    places = [(q, s) for q in range(3) for s in streams]
    total = forward(rows, [quarter[q][s] for q, s in places], places, None, F32)
    places = [(3, s) for s in streams]
    joined = forward(rows, quarter[3], places, total, BF16)
    grad = joined_grad_of(row_counts, joined[:row_total], swap_core(joined[row_total:]), target_rows, norm_gain)
    grads = jnp.concatenate([grad, swap_core(grad)], 0)

    def product(s, q):
        return jnp.dot(features[s, q * 256 : (q + 1) * 256], grads, preferred_element_type=F32)

    sent = [product(s, 3).astype(BF16) for s in streams]
    got3 = [swap(sent[s], ROUNDS[s][2]) for s in streams]
    sent = [product(s, 2).astype(BF16) for s in streams]
    got2 = [swap(sent[s], ROUNDS[s][2]) for s in streams]
    sent = [(product(s, 1) + got3[s].astype(F32)).astype(BF16) for s in streams]
    got1 = [swap(sent[s], ROUNDS[s][1]) for s in streams]
    kept = [product(s, 0) + got2[s].astype(F32) + got1[s].astype(F32) for s in streams]
    got0 = [swap(kept[s][128:].astype(BF16), ROUNDS[s][0]) for s in streams]
    kept = [(kept[s][:128] + got0[s].astype(F32)).astype(BF16).reshape(8, 1, 16, width) for s in streams]
    near = jnp.concatenate(kept, 1).reshape(8 * 48, width)
    owned_grad = jnp.sum(cube_exchange(near).reshape(8, 48, width).astype(F32), axis=0)
    return normalize_rows(owned_grad).astype(BF16)


def solution(mesh):
    return jax.shard_map(
        local,
        mesh=mesh,
        in_specs=(
            P(("replica", "shard"), None),
            P(("replica", "shard")),
            P(("replica", "shard"), None),
            P(("replica", "shard"), None),
            P(),
        ),
        out_specs=P(("replica", "shard"), None),
        check_vma=False,
    )
```

```python
import jax
import jax.numpy as jnp
from jax import lax
from jax.experimental import pallas as pl
from jax.experimental.pallas import tpu as pltpu
from jax.sharding import PartitionSpec as P

epsilon = 1e-06
AXES = ("replica", "shard")
STRIDE = {"z": 16, "y": 4, "x": 1}
ROUNDS = (("z", "y", "x"), ("x", "z", "y"), ("y", "x", "z"))
F32, BF16 = jnp.float32, jnp.bfloat16


def half_place(a, core):
    if core == 0:
        return a // 2, a % 2
    return (a + 1) // 2 % 2, a // 2


def chips():
    return [(z, y, x) for z in range(4) for y in range(4) for x in range(4)]


def device(z, y, x, core):
    return (z * 16 + y * 4 + x) * 2 + core


def cubes():
    groups = {}
    for z, y, x in chips():
        for core in range(2):
            halves, places = zip(*(half_place(a, core) for a in (z, y, x)))
            groups.setdefault((core, halves), {})[places] = device(z, y, x, core)
    return [[members[k] for k in sorted(members)] for members in groups.values()]


def swap_pairs(axis):
    pairs = []
    for r in range(64):
        for core in range(2):
            a = r // STRIDE[axis] % 4
            other = r + ((a ^ (3 if core == 0 else 1)) - a) * STRIDE[axis]
            pairs.append((r * 2 + core, other * 2 + core))
    return pairs


def swap(value, axis):
    return lax.ppermute(value, AXES, swap_pairs(axis))


def swap_core(value):
    return lax.ppermute(value, "shard", [(0, 1), (1, 0)])


def cube_exchange(value):
    return lax.all_to_all(value, AXES, 0, 0, axis_index_groups=cubes(), tiled=True)


def arrange_kernel(own_ref, other_ref, out_ref):
    step = pl.program_id(0)
    replica, core = lax.axis_index("replica"), lax.axis_index("shard")
    mine = {"z": replica // 16, "y": replica // 4 % 4, "x": replica % 4}
    m = own_ref.shape[0]
    turned = [own_ref[...].T, other_ref[...].T]
    for x in range(4):
        at = {"z": step // 4, "y": step % 4, "x": x}
        slots, orders = [], []
        for owner in range(2):
            flip, place = {}, {}
            for axis in "zyx":
                half, place[axis] = half_place(at[axis], owner)
                own_half, _ = half_place(mine[axis], owner)
                flip[axis] = lax.rem(half + own_half, 2)
            slots.append(place["z"] * 4 + place["y"] * 2 + place["x"])
            orders.append([flip[order[0]] + 2 * flip[order[1]] + 4 * flip[order[2]] for order in ROUNDS])
        slot = jnp.where(core == 0, *slots)
        chunks = [jnp.where(core == 0, *pair) for pair in zip(*orders)]
        for third in range(3):
            near = slot * 3 + third
            s = near // 8
            chunk = jnp.where(s == 0, chunks[0], jnp.where(s == 1, chunks[1], chunks[2]))
            first = (x * 6 + third) * 16
            for part, value in enumerate(turned):
                tile = jnp.where(core == 0, value[first : first + 16], value[first + 48 : first + 64])
                out_ref[s, chunk, lax.rem(near, 8), :, part * m : (part + 1) * m] = tile


def arrange(own_rows, other_rows):
    m = own_rows.shape[0]
    shape = (3, 8, 8, 16, 2 * m)
    out = pl.pallas_call(
        arrange_kernel,
        grid=(16,),
        in_specs=[pl.BlockSpec((m, 384), lambda i: (0, i))] * 2,
        out_specs=pl.BlockSpec(shape, lambda i: (0,) * 5),
        out_shape=jax.ShapeDtypeStruct(shape, BF16),
        compiler_params=pltpu.CompilerParams(vmem_limit_bytes=32 << 20),
        cost_estimate=pl.CostEstimate(flops=0, bytes_accessed=1024, transcendentals=0),
    )(own_rows, other_rows)
    return out.reshape(3, 1024, 2 * m)


def turn_kernel(in_ref, out_ref):
    out_ref[0] = in_ref[0].T


def turn(features):
    streams, k, m = features.shape
    return pl.pallas_call(
        turn_kernel,
        grid=(streams, 2),
        in_specs=[pl.BlockSpec((1, k // 2, m), lambda i, j: (i, j, 0))],
        out_specs=pl.BlockSpec((1, m, k // 2), lambda i, j: (i, 0, j)),
        out_shape=jax.ShapeDtypeStruct((streams, m, k), BF16),
        compiler_params=pltpu.CompilerParams(vmem_limit_bytes=32 << 20),
        cost_estimate=pl.CostEstimate(flops=0, bytes_accessed=1024, transcendentals=0),
    )(features)


def forward(rows, pieces, places, added, half, dtypes):
    m, width, cols = rows.shape[1] // 2, pieces[0].shape[1], 512
    n, e = len(pieces), len(added)
    halves = (0, 1) if half is None else (half,)

    def kernel(*refs):
        rows_ref, outs = refs[0], refs[1 + n + e :]
        for h, out_ref in enumerate(outs):
            total = None
            for (q, s), piece in zip(places, refs[1 : 1 + n]):
                left = rows_ref[s, h * m : (h + 1) * m, q * 256 : (q + 1) * 256]
                part = jnp.dot(left, piece[...], preferred_element_type=F32)
                total = part if total is None else total + part
            for ref in refs[1 + n + h : 1 + n + e : len(halves)]:
                total = total + ref[...].astype(F32)
            out_ref[...] = total.astype(out_ref.dtype)

    block = pl.BlockSpec((m, cols), lambda j: (0, j))
    return pl.pallas_call(
        kernel,
        grid=(width // cols,),
        in_specs=[pl.BlockSpec((3, m * len(halves), 1024), lambda j: (0, half or 0, 0))]
        + [pl.BlockSpec((256, cols), lambda j: (0, j))] * n
        + [block] * e,
        out_specs=[block] * len(halves),
        out_shape=[jax.ShapeDtypeStruct((m, width), dtype) for dtype in dtypes],
        compiler_params=pltpu.CompilerParams(vmem_limit_bytes=40 << 20),
        cost_estimate=pl.CostEstimate(
            flops=2 * m * len(halves) * 256 * n * width, bytes_accessed=n * 512 * width + 4 * (e + 2) * m * width, transcendentals=0
        ),
    )(rows, *pieces, *added)


def grad_kernel(count_ref, own_ref, other_ref, target_ref, gain_ref, out_ref):
    tile = out_ref.shape[0]
    row = lax.broadcasted_iota(jnp.int32, (tile, 1), 0) + pl.program_id(0) * tile
    live = (row < count_ref[0]).astype(F32)
    joined = own_ref[...].astype(F32) + other_ref[...].astype(F32)
    gain = gain_ref[...]
    inverse = lax.rsqrt(jnp.mean(joined * joined, axis=1, keepdims=True) + epsilon)
    normed = joined * inverse
    error = live * (normed * gain - target_ref[...].astype(F32))
    scaled = error * gain
    mean = jnp.mean(scaled * normed, axis=1, keepdims=True)
    out_ref[...] = (inverse * (scaled - normed * mean)).astype(BF16)


def joined_grad_of(row_counts, own, other, target_rows, norm_gain):
    rows, width = target_rows.shape
    tile = 64
    block = pl.BlockSpec((tile, width), lambda i: (i, 0))
    return pl.pallas_call(
        grad_kernel,
        grid=(rows // tile,),
        in_specs=[pl.BlockSpec(memory_space=pltpu.SMEM), block, block, block, pl.BlockSpec((1, width), lambda i: (0, 0))],
        out_specs=block,
        out_shape=jax.ShapeDtypeStruct((rows, width), BF16),
        compiler_params=pltpu.CompilerParams(vmem_limit_bytes=32 << 20),
        cost_estimate=pl.CostEstimate(flops=12 * rows * width, bytes_accessed=8 * rows * width, transcendentals=rows),
    )(row_counts, own, other, target_rows, norm_gain.reshape(1, width))


def normalize_rows(values):
    return -values * lax.rsqrt(jnp.mean(values * values, axis=-1, keepdims=True) + epsilon)


def local(hidden_rows, row_counts, target_rows, joined_weight, norm_gain):
    row_total, width = target_rows.shape
    streams = range(3)

    with jax.named_scope("cube"):
        away_rows = swap_core(hidden_rows)
        sent, hidden_rows = lax.optimization_barrier((jnp.tile(joined_weight, (8, 1)), hidden_rows))
        near = cube_exchange(sent)
    with jax.named_scope("arrange"):
        features = arrange(hidden_rows, away_rows)
        rows = turn(features)
        near, features, rows = lax.optimization_barrier((near, features, rows))
    first = [near[128 * s : 128 * (s + 1)] for s in streams]
    second, quarter = [None] * 3, [[None] * 3 for _ in range(4)]
    for s in streams:
        with jax.named_scope(f"gather_a{s}"):
            second[s] = swap(first[s], ROUNDS[s][0])
            quarter[0][s] = jnp.concatenate([first[s], second[s]], 0)
    for s in streams:
        with jax.named_scope(f"gather_b{s}"):
            quarter[1][s] = swap(quarter[0][s], ROUNDS[s][1])
    for s in streams:
        with jax.named_scope(f"gather_c{s}"):
            quarter[2][s] = swap(quarter[0][s], ROUNDS[s][2])
        with jax.named_scope(f"gather_d{s}"):
            quarter[3][s] = swap(quarter[1][s], ROUNDS[s][2])

    def step(quarters, added, half, dtypes):
        places = [(q, s) for q in quarters for s in streams]
        return forward(rows, [quarter[q][s] for q, s in places], places, added, half, dtypes)

    with jax.named_scope("forward0"):
        part = step((0, 1), [], None, (F32, F32))
    with jax.named_scope("forward1"):
        own, away = step((2,), part, None, (F32, BF16))
        own_rest = swap_core(away)
    with jax.named_scope("forward2"):
        (away,) = step((3,), [], 1, (BF16,))
        other = swap_core(away)
    with jax.named_scope("forward3"):
        (own,) = step((3,), [own, own_rest], 0, (F32,))
    with jax.named_scope("grad"):
        grad = joined_grad_of(row_counts, own, other, target_rows, norm_gain)
        other_grad = swap_core(grad)
        grads = jnp.concatenate([grad, other_grad], 0)

    def product(s, q):
        return jnp.dot(features[s, q * 256 : (q + 1) * 256], grads, preferred_element_type=F32)

    got, kept = [[None] * 3 for _ in range(4)], []
    for s in streams:
        with jax.named_scope(f"reduce_d{s}"):
            got[3][s] = swap(product(s, 3).astype(BF16), ROUNDS[s][2])
    for s in streams:
        with jax.named_scope(f"reduce_c{s}"):
            got[2][s] = swap(product(s, 2).astype(BF16), ROUNDS[s][2])
    for s in streams:
        with jax.named_scope(f"reduce_b{s}"):
            got[1][s] = swap((product(s, 1) + got[3][s].astype(F32)).astype(BF16), ROUNDS[s][1])
    for s in streams:
        with jax.named_scope(f"reduce_a{s}"):
            part = product(s, 0) + got[2][s].astype(F32) + got[1][s].astype(F32)
            got[0][s] = swap(part[128:].astype(BF16), ROUNDS[s][0])
            kept.append((part[:128] + got[0][s].astype(F32)).astype(BF16))
    near = jnp.concatenate(kept, 0)
    owned_grad = jnp.sum(cube_exchange(near).reshape(8, 48, width).astype(F32), axis=0)
    return normalize_rows(owned_grad).astype(BF16)


def solution(mesh):
    return jax.shard_map(
        local,
        mesh=mesh,
        in_specs=(
            P(("replica", "shard"), None),
            P(("replica", "shard")),
            P(("replica", "shard"), None),
            P(("replica", "shard"), None),
            P(),
        ),
        out_specs=P(("replica", "shard"), None),
        check_vma=False,
    )
```

```python
import jax
import jax.numpy as jnp
from jax import lax
from jax.experimental import pallas as pl
from jax.experimental.pallas import tpu as pltpu
from jax.sharding import PartitionSpec as P

epsilon = 1e-06
AXES = ("replica", "shard")
STRIDE = {"z": 16, "y": 4, "x": 1}
ROUNDS = (("y", "z", "x"), ("x", "y", "z"), ("z", "x", "y"))
LONG = ('zyx', '')
F32, BF16 = jnp.float32, jnp.bfloat16


def half_place(a, axis, core):
    if axis in LONG[core]:
        return a // 2, a % 2
    return (a + 1) // 2 % 2, a // 2


def chips():
    return [(z, y, x) for z in range(4) for y in range(4) for x in range(4)]


def device(z, y, x, core):
    return (z * 16 + y * 4 + x) * 2 + core


def cubes():
    groups = {}
    for z, y, x in chips():
        for core in range(2):
            halves, places = zip(*(half_place(a, axis, core) for axis, a in zip("zyx", (z, y, x))))
            groups.setdefault((core, halves), {})[places] = device(z, y, x, core)
    return [[members[k] for k in sorted(members)] for members in groups.values()]


def swap_pairs(axis):
    pairs = []
    for r in range(64):
        for core in range(2):
            a = r // STRIDE[axis] % 4
            other = r + ((a ^ (3 if axis in LONG[core] else 1)) - a) * STRIDE[axis]
            pairs.append((r * 2 + core, other * 2 + core))
    return pairs


def swap(value, axis):
    return lax.ppermute(value, AXES, swap_pairs(axis))


def swap_core(value):
    return lax.ppermute(value, "shard", [(0, 1), (1, 0)])


def cube_exchange(value):
    return lax.all_to_all(value, AXES, 0, 0, axis_index_groups=cubes(), tiled=True)


def arrange_kernel(own_ref, other_ref, out_ref):
    z = pl.program_id(0)
    replica, core = lax.axis_index("replica"), lax.axis_index("shard")
    mine = {"z": replica // 16, "y": replica // 4 % 4, "x": replica % 4}
    m = own_ref.shape[0]
    row = lax.broadcasted_iota(jnp.int32, (192, 384), 0)
    block = (row >= 48).astype(jnp.int32) + (row >= 96).astype(jnp.int32) + (row >= 144).astype(jnp.int32)
    pick = lax.broadcasted_iota(jnp.int32, (192, 384), 1) == row + 48 * (block + core)
    pick = pick.astype(F32).astype(BF16)
    for y in range(4):
        turned = []
        for ref in (own_ref, other_ref):
            value = ref[:, 384 * y : 384 * (y + 1)]
            turned.append(lax.dot_general(pick, value, (((1,), (1,)), ((), ())), preferred_element_type=F32).astype(BF16))
        for x in range(4):
            at = {"z": z, "y": y, "x": x}
            slots, orders = [], []
            for owner in range(2):
                flip, place = {}, {}
                for axis in "zyx":
                    half, place[axis] = half_place(at[axis], axis, owner)
                    own_half, _ = half_place(mine[axis], axis, owner)
                    flip[axis] = lax.rem(half + own_half, 2)
                slots.append(place["z"] * 4 + place["y"] * 2 + place["x"])
                orders.append([flip[order[0]] + 2 * flip[order[1]] + 4 * flip[order[2]] for order in ROUNDS])
            slot = jnp.where(core == 0, *slots)
            chunks = [jnp.where(core == 0, *pair) for pair in zip(*orders)]
            for third in range(3):
                near = slot * 3 + third
                s = near // 8
                chunk = jnp.where(s == 0, chunks[0], jnp.where(s == 1, chunks[1], chunks[2]))
                first = (x * 3 + third) * 16
                for part, value in enumerate(turned):
                    out_ref[s, chunk, lax.rem(near, 8), :, part * m : (part + 1) * m] = value[first : first + 16]


def arrange(own_rows, other_rows):
    m = own_rows.shape[0]
    shape = (3, 8, 8, 16, 2 * m)
    out = pl.pallas_call(
        arrange_kernel,
        grid=(4,),
        in_specs=[pl.BlockSpec((m, 1536), lambda i: (0, i))] * 2,
        out_specs=pl.BlockSpec(shape, lambda i: (0,) * 5),
        out_shape=jax.ShapeDtypeStruct(shape, BF16),
        compiler_params=pltpu.CompilerParams(vmem_limit_bytes=32 << 20),
        cost_estimate=pl.CostEstimate(flops=0, bytes_accessed=1024, transcendentals=0),
    )(own_rows, other_rows)
    return out.reshape(3, 1024, 2 * m)


def turn_kernel(in_ref, out_ref):
    out_ref[0] = in_ref[0].T


def turn(features):
    streams, k, m = features.shape
    return pl.pallas_call(
        turn_kernel,
        grid=(streams, 2),
        in_specs=[pl.BlockSpec((1, k // 2, m), lambda i, j: (i, j, 0))],
        out_specs=pl.BlockSpec((1, m, k // 2), lambda i, j: (i, 0, j)),
        out_shape=jax.ShapeDtypeStruct((streams, m, k), BF16),
        compiler_params=pltpu.CompilerParams(vmem_limit_bytes=32 << 20),
        cost_estimate=pl.CostEstimate(flops=0, bytes_accessed=1024, transcendentals=0),
    )(features)


def forward(rows, pieces, places, added, half, dtypes):
    m, width, cols = rows.shape[1] // 2, pieces[0].shape[1], 512 if half is None else 1024
    n, e = len(pieces), len(added)
    halves = (0, 1) if half is None else (half,)

    def kernel(*refs):
        rows_ref, outs = refs[0], refs[1 + n + e :]
        for h, out_ref in enumerate(outs):
            total = None
            for (q, s), piece in zip(places, refs[1 : 1 + n]):
                left = rows_ref[s, h * m : (h + 1) * m, q * 256 : (q + 1) * 256]
                part = jnp.dot(left, piece[...], preferred_element_type=F32)
                total = part if total is None else total + part
            for ref in refs[1 + n + h : 1 + n + e : len(halves)]:
                total = total + ref[...].astype(F32)
            out_ref[...] = total.astype(out_ref.dtype)

    block = pl.BlockSpec((m, cols), lambda j: (0, j))
    return pl.pallas_call(
        kernel,
        grid=(width // cols,),
        in_specs=[pl.BlockSpec((3, m * len(halves), 1024), lambda j: (0, half or 0, 0))]
        + [pl.BlockSpec((256, cols), lambda j: (0, j))] * n
        + [block] * e,
        out_specs=[block] * len(halves),
        out_shape=[jax.ShapeDtypeStruct((m, width), dtype) for dtype in dtypes],
        compiler_params=pltpu.CompilerParams(vmem_limit_bytes=40 << 20),
        cost_estimate=pl.CostEstimate(
            flops=2 * m * len(halves) * 256 * n * width, bytes_accessed=n * 512 * width + 4 * (e + 2) * m * width, transcendentals=0
        ),
    )(rows, *pieces, *added)


def grad_kernel(count_ref, own_ref, other_ref, target_ref, gain_ref, out_ref):
    rows, width = out_ref.shape
    tile = 64
    gain = gain_ref[...]

    @pl.loop(0, rows // tile)
    def _(i):
        at = pl.ds(pl.multiple_of(i * tile, tile), tile)
        row = lax.broadcasted_iota(jnp.int32, (tile, 1), 0) + i * tile
        live = (row < count_ref[0]).astype(F32)
        joined = own_ref[at, :].astype(F32) + other_ref[at, :].astype(F32)
        inverse = lax.rsqrt(jnp.mean(joined * joined, axis=1, keepdims=True) + epsilon)
        normed = joined * inverse
        error = live * (normed * gain - target_ref[at, :].astype(F32))
        scaled = error * gain
        mean = jnp.mean(scaled * normed, axis=1, keepdims=True)
        out_ref[at, :] = (inverse * (scaled - normed * mean)).astype(BF16)


def joined_grad_of(row_counts, own, other, target_rows, norm_gain):
    rows, width = target_rows.shape
    whole = pl.BlockSpec(memory_space=pltpu.VMEM)
    return pl.pallas_call(
        grad_kernel,
        in_specs=[pl.BlockSpec(memory_space=pltpu.SMEM)] + [whole] * 4,
        out_specs=whole,
        out_shape=jax.ShapeDtypeStruct((rows, width), BF16),
        compiler_params=pltpu.CompilerParams(vmem_limit_bytes=32 << 20),
        cost_estimate=pl.CostEstimate(flops=12 * rows * width, bytes_accessed=8 * rows * width, transcendentals=rows),
    )(row_counts, own, other, target_rows, norm_gain.reshape(1, width))


def normalize_rows(values):
    return -values * lax.rsqrt(jnp.mean(values * values, axis=-1, keepdims=True) + epsilon)


def local(hidden_rows, row_counts, target_rows, joined_weight, norm_gain):
    row_total, width = target_rows.shape
    streams = range(3)

    with jax.named_scope("cube"):
        away_rows = swap_core(hidden_rows)
        sent, hidden_rows = lax.optimization_barrier((jnp.tile(joined_weight, (8, 1)), hidden_rows))
        near = cube_exchange(sent)
    with jax.named_scope("arrange"):
        features = arrange(hidden_rows, away_rows)
        rows = turn(features)
        near, features, rows = lax.optimization_barrier((near, features, rows))
    first = [near[128 * s : 128 * (s + 1)] for s in streams]
    second, quarter = [None] * 3, [[None] * 3 for _ in range(4)]
    for s in streams:
        with jax.named_scope(f"gather_a{s}"):
            second[s] = swap(first[s], ROUNDS[s][0])
            quarter[0][s] = jnp.concatenate([first[s], second[s]], 0)
    for s in streams:
        with jax.named_scope(f"gather_b{s}"):
            quarter[1][s] = swap(quarter[0][s], ROUNDS[s][1])
    for s in streams:
        with jax.named_scope(f"gather_c{s}"):
            quarter[2][s] = swap(quarter[0][s], ROUNDS[s][2])
        with jax.named_scope(f"gather_d{s}"):
            quarter[3][s] = swap(quarter[1][s], ROUNDS[s][2])

    def step(quarters, added, half, dtypes):
        places = [(q, s) for q in quarters for s in streams]
        return forward(rows, [quarter[q][s] for q, s in places], places, added, half, dtypes)

    with jax.named_scope("forward0"):
        part = step((0, 1), [], None, (F32, F32))
    with jax.named_scope("forward1"):
        own, away = step((2,), part, None, (F32, BF16))
        own_rest = swap_core(away)
    with jax.named_scope("forward2"):
        (away,) = step((3,), [], 1, (BF16,))
        other = swap_core(away)
    with jax.named_scope("forward3"):
        (own,) = step((3,), [own, own_rest], 0, (F32,))
    with jax.named_scope("grad"):
        grad = joined_grad_of(row_counts, own, other, target_rows, norm_gain)
        other_grad = swap_core(grad)
        grads = jnp.concatenate([grad, other_grad], 0)

    def product(s, q):
        return jnp.dot(features[s, q * 256 : (q + 1) * 256], grads, preferred_element_type=F32)

    got, kept = [[None] * 3 for _ in range(4)], []
    for s in streams:
        with jax.named_scope(f"reduce_d{s}"):
            got[3][s] = swap(product(s, 3).astype(BF16), ROUNDS[s][2])
    for s in streams:
        with jax.named_scope(f"reduce_c{s}"):
            got[2][s] = swap(product(s, 2).astype(BF16), ROUNDS[s][2])
    for s in streams:
        with jax.named_scope(f"reduce_b{s}"):
            got[1][s] = swap((product(s, 1) + got[3][s].astype(F32)).astype(BF16), ROUNDS[s][1])
    for s in streams:
        with jax.named_scope(f"reduce_a{s}"):
            part = product(s, 0) + got[2][s].astype(F32) + got[1][s].astype(F32)
            got[0][s] = swap(part[128:].astype(BF16), ROUNDS[s][0])
            kept.append((part[:128] + got[0][s].astype(F32)).astype(BF16))
    near = jnp.concatenate(kept, 0)
    owned_grad = jnp.sum(cube_exchange(near).reshape(8, 48, width).astype(F32), axis=0)
    return normalize_rows(owned_grad).astype(BF16)


def solution(mesh):
    return jax.shard_map(
        local,
        mesh=mesh,
        in_specs=(
            P(("replica", "shard"), None),
            P(("replica", "shard")),
            P(("replica", "shard"), None),
            P(("replica", "shard"), None),
            P(),
        ),
        out_specs=P(("replica", "shard"), None),
        check_vma=False,
    )
```

```python
import jax
import jax.numpy as jnp
from jax import lax
from jax.experimental import pallas as pl
from jax.experimental.pallas import tpu as pltpu
from jax.sharding import PartitionSpec as P

epsilon = 1e-06
AXES = ("replica", "shard")
STRIDE = {"z": 16, "y": 4, "x": 1}
ROUNDS = (("y", "z", "x"), ("x", "y", "z"), ("z", "x", "y"))
LONG = ('zy', 'x')
F32, BF16 = jnp.float32, jnp.bfloat16


def half_place(a, axis, core):
    if axis in LONG[core]:
        return a // 2, a % 2
    return (a + 1) // 2 % 2, a // 2


def chips():
    return [(z, y, x) for z in range(4) for y in range(4) for x in range(4)]


def device(z, y, x, core):
    return (z * 16 + y * 4 + x) * 2 + core


def cubes():
    groups = {}
    for z, y, x in chips():
        for core in range(2):
            halves, places = zip(*(half_place(a, axis, core) for axis, a in zip("zyx", (z, y, x))))
            groups.setdefault((core, halves), {})[places] = device(z, y, x, core)
    return [[members[k] for k in sorted(members)] for members in groups.values()]


def swap_pairs(axis):
    pairs = []
    for r in range(64):
        for core in range(2):
            a = r // STRIDE[axis] % 4
            other = r + ((a ^ (3 if axis in LONG[core] else 1)) - a) * STRIDE[axis]
            pairs.append((r * 2 + core, other * 2 + core))
    return pairs


def swap(value, axis):
    return lax.ppermute(value, AXES, swap_pairs(axis))


def swap_core(value):
    return lax.ppermute(value, "shard", [(0, 1), (1, 0)])


def cube_exchange(value):
    return lax.all_to_all(value, AXES, 0, 0, axis_index_groups=cubes(), tiled=True)


def arrange_kernel(own_ref, other_ref, out_ref):
    z = pl.program_id(0)
    replica, core = lax.axis_index("replica"), lax.axis_index("shard")
    mine = {"z": replica // 16, "y": replica // 4 % 4, "x": replica % 4}
    m = own_ref.shape[0]
    row = lax.broadcasted_iota(jnp.int32, (192, 384), 0)
    block = (row >= 48).astype(jnp.int32) + (row >= 96).astype(jnp.int32) + (row >= 144).astype(jnp.int32)
    pick = lax.broadcasted_iota(jnp.int32, (192, 384), 1) == row + 48 * (block + core)
    pick = pick.astype(F32).astype(BF16)
    for y in range(4):
        turned = []
        for ref in (own_ref, other_ref):
            value = ref[:, 384 * y : 384 * (y + 1)]
            turned.append(lax.dot_general(pick, value, (((1,), (1,)), ((), ())), preferred_element_type=F32).astype(BF16))
        for x in range(4):
            at = {"z": z, "y": y, "x": x}
            slots, orders = [], []
            for owner in range(2):
                flip, place = {}, {}
                for axis in "zyx":
                    half, place[axis] = half_place(at[axis], axis, owner)
                    own_half, _ = half_place(mine[axis], axis, owner)
                    flip[axis] = lax.rem(half + own_half, 2)
                slots.append(place["z"] * 4 + place["y"] * 2 + place["x"])
                orders.append([flip[order[0]] + 2 * flip[order[1]] + 4 * flip[order[2]] for order in ROUNDS])
            slot = jnp.where(core == 0, *slots)
            chunks = [jnp.where(core == 0, *pair) for pair in zip(*orders)]
            for third in range(3):
                near = slot * 3 + third
                s = near // 8
                chunk = jnp.where(s == 0, chunks[0], jnp.where(s == 1, chunks[1], chunks[2]))
                first = (x * 3 + third) * 16
                for part, value in enumerate(turned):
                    out_ref[s, chunk, lax.rem(near, 8), :, part * m : (part + 1) * m] = value[first : first + 16]


def arrange(own_rows, other_rows):
    m = own_rows.shape[0]
    shape = (3, 8, 8, 16, 2 * m)
    out = pl.pallas_call(
        arrange_kernel,
        grid=(4,),
        in_specs=[pl.BlockSpec((m, 1536), lambda i: (0, i))] * 2,
        out_specs=pl.BlockSpec(shape, lambda i: (0,) * 5),
        out_shape=jax.ShapeDtypeStruct(shape, BF16),
        compiler_params=pltpu.CompilerParams(vmem_limit_bytes=32 << 20),
        cost_estimate=pl.CostEstimate(flops=0, bytes_accessed=1024, transcendentals=0),
    )(own_rows, other_rows)
    return out.reshape(3, 1024, 2 * m)


def turn_kernel(in_ref, out_ref):
    out_ref[0] = in_ref[0].T


def turn(features):
    streams, k, m = features.shape
    return pl.pallas_call(
        turn_kernel,
        grid=(streams, 2),
        in_specs=[pl.BlockSpec((1, k // 2, m), lambda i, j: (i, j, 0))],
        out_specs=pl.BlockSpec((1, m, k // 2), lambda i, j: (i, 0, j)),
        out_shape=jax.ShapeDtypeStruct((streams, m, k), BF16),
        compiler_params=pltpu.CompilerParams(vmem_limit_bytes=32 << 20),
        cost_estimate=pl.CostEstimate(flops=0, bytes_accessed=1024, transcendentals=0),
    )(features)


def forward(rows, pieces, places, added, half, dtypes):
    m, width, cols = rows.shape[1] // 2, pieces[0].shape[1], 512 if half is None else 1024
    n, e = len(pieces), len(added)
    halves = (0, 1) if half is None else (half,)

    def kernel(*refs):
        rows_ref, outs = refs[0], refs[1 + n + e :]
        for h, out_ref in enumerate(outs):
            total = None
            for (q, s), piece in zip(places, refs[1 : 1 + n]):
                left = rows_ref[s, h * m : (h + 1) * m, q * 256 : (q + 1) * 256]
                part = jnp.dot(left, piece[...], preferred_element_type=F32)
                total = part if total is None else total + part
            for ref in refs[1 + n + h : 1 + n + e : len(halves)]:
                total = total + ref[...].astype(F32)
            out_ref[...] = total.astype(out_ref.dtype)

    block = pl.BlockSpec((m, cols), lambda j: (0, j))
    return pl.pallas_call(
        kernel,
        grid=(width // cols,),
        in_specs=[pl.BlockSpec((3, m * len(halves), 1024), lambda j: (0, half or 0, 0))]
        + [pl.BlockSpec((256, cols), lambda j: (0, j))] * n
        + [block] * e,
        out_specs=[block] * len(halves),
        out_shape=[jax.ShapeDtypeStruct((m, width), dtype) for dtype in dtypes],
        compiler_params=pltpu.CompilerParams(vmem_limit_bytes=40 << 20),
        cost_estimate=pl.CostEstimate(
            flops=2 * m * len(halves) * 256 * n * width, bytes_accessed=n * 512 * width + 4 * (e + 2) * m * width, transcendentals=0
        ),
    )(rows, *pieces, *added)


def grad_kernel(count_ref, own_ref, other_ref, target_ref, gain_ref, out_ref):
    rows, width = out_ref.shape
    tile = 64
    gain = gain_ref[...]

    @pl.loop(0, rows // tile)
    def _(i):
        at = pl.ds(pl.multiple_of(i * tile, tile), tile)
        row = lax.broadcasted_iota(jnp.int32, (tile, 1), 0) + i * tile
        live = (row < count_ref[0]).astype(F32)
        joined = own_ref[at, :].astype(F32) + other_ref[at, :].astype(F32)
        inverse = lax.rsqrt(jnp.mean(joined * joined, axis=1, keepdims=True) + epsilon)
        normed = joined * inverse
        error = live * (normed * gain - target_ref[at, :].astype(F32))
        scaled = error * gain
        mean = jnp.mean(scaled * normed, axis=1, keepdims=True)
        out_ref[at, :] = (inverse * (scaled - normed * mean)).astype(BF16)


def joined_grad_of(row_counts, own, other, target_rows, norm_gain):
    rows, width = target_rows.shape
    whole = pl.BlockSpec(memory_space=pltpu.VMEM)
    return pl.pallas_call(
        grad_kernel,
        in_specs=[pl.BlockSpec(memory_space=pltpu.SMEM)] + [whole] * 4,
        out_specs=whole,
        out_shape=jax.ShapeDtypeStruct((rows, width), BF16),
        compiler_params=pltpu.CompilerParams(vmem_limit_bytes=32 << 20),
        cost_estimate=pl.CostEstimate(flops=12 * rows * width, bytes_accessed=8 * rows * width, transcendentals=rows),
    )(row_counts, own, other, target_rows, norm_gain.reshape(1, width))


def normalize_rows(values):
    return -values * lax.rsqrt(jnp.mean(values * values, axis=-1, keepdims=True) + epsilon)


def local(hidden_rows, row_counts, target_rows, joined_weight, norm_gain):
    row_total, width = target_rows.shape
    streams = range(3)

    with jax.named_scope("cube"):
        away_rows = swap_core(hidden_rows)
        sent, hidden_rows = lax.optimization_barrier((jnp.tile(joined_weight, (8, 1)), hidden_rows))
        near = cube_exchange(sent)
    with jax.named_scope("arrange"):
        features = arrange(hidden_rows, away_rows)
        rows = turn(features)
        near, features, rows = lax.optimization_barrier((near, features, rows))
    first = [near[128 * s : 128 * (s + 1)] for s in streams]
    second, quarter = [None] * 3, [[None] * 3 for _ in range(4)]
    for s in streams:
        with jax.named_scope(f"gather_a{s}"):
            second[s] = swap(first[s], ROUNDS[s][0])
            quarter[0][s] = jnp.concatenate([first[s], second[s]], 0)
    for s in streams:
        with jax.named_scope(f"gather_b{s}"):
            quarter[1][s] = swap(quarter[0][s], ROUNDS[s][1])
    for s in streams:
        with jax.named_scope(f"gather_c{s}"):
            quarter[2][s] = swap(quarter[0][s], ROUNDS[s][2])
        with jax.named_scope(f"gather_d{s}"):
            quarter[3][s] = swap(quarter[1][s], ROUNDS[s][2])

    def step(quarters, added, half, dtypes):
        places = [(q, s) for q in quarters for s in streams]
        return forward(rows, [quarter[q][s] for q, s in places], places, added, half, dtypes)

    with jax.named_scope("forward0"):
        part = step((0, 1), [], None, (F32, F32))
    with jax.named_scope("forward1"):
        own, away = step((2,), part, None, (F32, BF16))
        own_rest = swap_core(away)
    with jax.named_scope("forward2"):
        (away,) = step((3,), [], 1, (BF16,))
        other = swap_core(away)
    with jax.named_scope("forward3"):
        (own,) = step((3,), [own, own_rest], 0, (F32,))
    with jax.named_scope("grad"):
        grad = joined_grad_of(row_counts, own, other, target_rows, norm_gain)
        other_grad = swap_core(grad)
        grads = jnp.concatenate([grad, other_grad], 0)

    def product(s, q):
        return jnp.dot(features[s, q * 256 : (q + 1) * 256], grads, preferred_element_type=F32)

    got, kept = [[None] * 3 for _ in range(4)], []
    for s in streams:
        with jax.named_scope(f"reduce_d{s}"):
            got[3][s] = swap(product(s, 3).astype(BF16), ROUNDS[s][2])
    for s in streams:
        with jax.named_scope(f"reduce_c{s}"):
            got[2][s] = swap(product(s, 2).astype(BF16), ROUNDS[s][2])
    for s in streams:
        with jax.named_scope(f"reduce_b{s}"):
            got[1][s] = swap((product(s, 1) + got[3][s].astype(F32)).astype(BF16), ROUNDS[s][1])
    for s in streams:
        with jax.named_scope(f"reduce_a{s}"):
            part = product(s, 0) + got[2][s].astype(F32) + got[1][s].astype(F32)
            got[0][s] = swap(part[128:].astype(BF16), ROUNDS[s][0])
            kept.append((part[:128] + got[0][s].astype(F32)).astype(BF16))
    near = jnp.concatenate(kept, 0)
    owned_grad = jnp.sum(cube_exchange(near).reshape(8, 48, width).astype(F32), axis=0)
    return normalize_rows(owned_grad).astype(BF16)


def solution(mesh):
    return jax.shard_map(
        local,
        mesh=mesh,
        in_specs=(
            P(("replica", "shard"), None),
            P(("replica", "shard")),
            P(("replica", "shard"), None),
            P(("replica", "shard"), None),
            P(),
        ),
        out_specs=P(("replica", "shard"), None),
        check_vma=False,
    )
```

```python
import functools

import jax
import jax.numpy as jnp
from jax import lax
from jax.experimental import pallas as pl
from jax.experimental.pallas import tpu as pltpu
from jax.sharding import PartitionSpec as P

epsilon = 1e-06
AXES = ("replica", "shard")
STRIDE = {"z": 16, "y": 4, "x": 1}
ROUNDS = (("y", "z", "x"), ("x", "y", "z"), ("z", "x", "y"))
LONG = ('zy', 'x')
F32, BF16 = jnp.float32, jnp.bfloat16


def half_place(a, axis, core):
    if axis in LONG[core]:
        return a // 2, a % 2
    return (a + 1) // 2 % 2, a // 2


def chips():
    return [(z, y, x) for z in range(4) for y in range(4) for x in range(4)]


def device(z, y, x, core):
    return (z * 16 + y * 4 + x) * 2 + core


def cubes():
    groups = {}
    for z, y, x in chips():
        for core in range(2):
            halves, places = zip(*(half_place(a, axis, core) for axis, a in zip("zyx", (z, y, x))))
            groups.setdefault((core, halves), {})[places] = device(z, y, x, core)
    return [[members[k] for k in sorted(members)] for members in groups.values()]


def swap_pairs(axis):
    pairs = []
    for r in range(64):
        for core in range(2):
            a = r // STRIDE[axis] % 4
            other = r + ((a ^ (3 if axis in LONG[core] else 1)) - a) * STRIDE[axis]
            pairs.append((r * 2 + core, other * 2 + core))
    return pairs


def swap(value, axis):
    return lax.ppermute(value, AXES, swap_pairs(axis))


def swap_core(value):
    return lax.ppermute(value, "shard", [(0, 1), (1, 0)])


def cube_exchange(value):
    return lax.all_to_all(value, AXES, 0, 0, axis_index_groups=cubes(), tiled=True)


def arrange_kernel(own_ref, other_ref, out_ref):
    z = pl.program_id(0)
    replica, core = lax.axis_index("replica"), lax.axis_index("shard")
    mine = {"z": replica // 16, "y": replica // 4 % 4, "x": replica % 4}
    m = own_ref.shape[0]
    row = lax.broadcasted_iota(jnp.int32, (192, 384), 0)
    block = (row >= 48).astype(jnp.int32) + (row >= 96).astype(jnp.int32) + (row >= 144).astype(jnp.int32)
    pick = lax.broadcasted_iota(jnp.int32, (192, 384), 1) == row + 48 * (block + core)
    pick = pick.astype(F32).astype(BF16)
    for y in range(4):
        turned = []
        for ref in (own_ref, other_ref):
            value = ref[:, 384 * y : 384 * (y + 1)]
            turned.append(lax.dot_general(pick, value, (((1,), (1,)), ((), ())), preferred_element_type=F32).astype(BF16))
        for x in range(4):
            at = {"z": z, "y": y, "x": x}
            slots, orders = [], []
            for owner in range(2):
                flip, place = {}, {}
                for axis in "zyx":
                    half, place[axis] = half_place(at[axis], axis, owner)
                    own_half, _ = half_place(mine[axis], axis, owner)
                    flip[axis] = lax.rem(half + own_half, 2)
                slots.append(place["z"] * 4 + place["y"] * 2 + place["x"])
                orders.append([flip[order[0]] + 2 * flip[order[1]] + 4 * flip[order[2]] for order in ROUNDS])
            slot = jnp.where(core == 0, *slots)
            chunks = [jnp.where(core == 0, *pair) for pair in zip(*orders)]
            for third in range(3):
                near = slot * 3 + third
                s = near // 8
                chunk = jnp.where(s == 0, chunks[0], jnp.where(s == 1, chunks[1], chunks[2]))
                first = (x * 3 + third) * 16
                for part, value in enumerate(turned):
                    out_ref[s, chunk, lax.rem(near, 8), :, part * m : (part + 1) * m] = value[first : first + 16]


def arrange(own_rows, other_rows):
    m = own_rows.shape[0]
    shape = (3, 8, 8, 16, 2 * m)
    out = pl.pallas_call(
        arrange_kernel,
        grid=(4,),
        in_specs=[pl.BlockSpec((m, 1536), lambda i: (0, i))] * 2,
        out_specs=pl.BlockSpec(shape, lambda i: (0,) * 5),
        out_shape=jax.ShapeDtypeStruct(shape, BF16),
        compiler_params=pltpu.CompilerParams(vmem_limit_bytes=32 << 20),
        cost_estimate=pl.CostEstimate(flops=0, bytes_accessed=1024, transcendentals=0),
    )(own_rows, other_rows)
    return out.reshape(3, 1024, 2 * m)


def turn_kernel(in_ref, out_ref):
    out_ref[0] = in_ref[0].T


def turn(features):
    streams, k, m = features.shape
    return pl.pallas_call(
        turn_kernel,
        grid=(streams, 2),
        in_specs=[pl.BlockSpec((1, k // 2, m), lambda i, j: (i, j, 0))],
        out_specs=pl.BlockSpec((1, m, k // 2), lambda i, j: (i, 0, j)),
        out_shape=jax.ShapeDtypeStruct((streams, m, k), BF16),
        compiler_params=pltpu.CompilerParams(vmem_limit_bytes=32 << 20),
        cost_estimate=pl.CostEstimate(flops=0, bytes_accessed=1024, transcendentals=0),
    )(features)


def forward(rows, pieces, places, added, half, dtypes):
    m, width, cols = rows.shape[1] // 2, pieces[0].shape[1], 512 if half is None else 1024
    n, e = len(pieces), len(added)
    halves = (0, 1) if half is None else (half,)

    def kernel(*refs):
        rows_ref, outs = refs[0], refs[1 + n + e :]
        for h, out_ref in enumerate(outs):
            total = None
            for (q, s), piece in zip(places, refs[1 : 1 + n]):
                left = rows_ref[s, h * m : (h + 1) * m, q * 256 : (q + 1) * 256]
                part = jnp.dot(left, piece[...], preferred_element_type=F32)
                total = part if total is None else total + part
            for ref in refs[1 + n + h : 1 + n + e : len(halves)]:
                total = total + ref[...].astype(F32)
            out_ref[...] = total.astype(out_ref.dtype)

    block = pl.BlockSpec((m, cols), lambda j: (0, j))
    return pl.pallas_call(
        kernel,
        grid=(width // cols,),
        in_specs=[pl.BlockSpec((3, m * len(halves), 1024), lambda j: (0, half or 0, 0))]
        + [pl.BlockSpec((256, cols), lambda j: (0, j))] * n
        + [block] * e,
        out_specs=[block] * len(halves),
        out_shape=[jax.ShapeDtypeStruct((m, width), dtype) for dtype in dtypes],
        compiler_params=pltpu.CompilerParams(vmem_limit_bytes=40 << 20),
        cost_estimate=pl.CostEstimate(
            flops=2 * m * len(halves) * 256 * n * width, bytes_accessed=n * 512 * width + 4 * (e + 2) * m * width, transcendentals=0
        ),
    )(rows, *pieces, *added)


def grad_kernel(first, count_ref, own_ref, other_ref, target_ref, gain_ref, out_ref):
    rows, width = out_ref.shape
    tile = 64
    gain = gain_ref[...]

    @pl.loop(0, rows // tile)
    def _(i):
        to = pl.ds(pl.multiple_of(i * tile, tile), tile)
        at = pl.ds(pl.multiple_of(first + i * tile, tile), tile)
        row = lax.broadcasted_iota(jnp.int32, (tile, 1), 0) + first + i * tile
        live = (row < count_ref[0]).astype(F32)
        joined = own_ref[at, :].astype(F32) + other_ref[at, :].astype(F32)
        inverse = lax.rsqrt(jnp.mean(joined * joined, axis=1, keepdims=True) + epsilon)
        normed = joined * inverse
        error = live * (normed * gain - target_ref[at, :].astype(F32))
        scaled = error * gain
        mean = jnp.mean(scaled * normed, axis=1, keepdims=True)
        out_ref[to, :] = (inverse * (scaled - normed * mean)).astype(BF16)


def joined_grad_of(first, row_counts, own, other, target_rows, norm_gain):
    rows, width = target_rows.shape[0] // 2, target_rows.shape[1]
    whole = pl.BlockSpec(memory_space=pltpu.VMEM)
    return pl.pallas_call(
        functools.partial(grad_kernel, first),
        in_specs=[pl.BlockSpec(memory_space=pltpu.SMEM)] + [whole] * 4,
        out_specs=whole,
        out_shape=jax.ShapeDtypeStruct((rows, width), BF16),
        compiler_params=pltpu.CompilerParams(vmem_limit_bytes=32 << 20),
        cost_estimate=pl.CostEstimate(flops=12 * rows * width, bytes_accessed=8 * rows * width, transcendentals=rows),
    )(row_counts, own, other, target_rows, norm_gain.reshape(1, width))


def normalize_rows(values):
    return -values * lax.rsqrt(jnp.mean(values * values, axis=-1, keepdims=True) + epsilon)


def local(hidden_rows, row_counts, target_rows, joined_weight, norm_gain):
    row_total, width = target_rows.shape
    streams = range(3)

    with jax.named_scope("cube"):
        away_rows = swap_core(hidden_rows)
        sent, hidden_rows = lax.optimization_barrier((jnp.tile(joined_weight, (8, 1)), hidden_rows))
        near = cube_exchange(sent)
    with jax.named_scope("arrange"):
        features = arrange(hidden_rows, away_rows)
        rows = turn(features)
        near, features, rows = lax.optimization_barrier((near, features, rows))
    first = [near[128 * s : 128 * (s + 1)] for s in streams]
    second, quarter = [None] * 3, [[None] * 3 for _ in range(4)]
    for s in streams:
        with jax.named_scope(f"gather_a{s}"):
            second[s] = swap(first[s], ROUNDS[s][0])
            quarter[0][s] = jnp.concatenate([first[s], second[s]], 0)
    for s in streams:
        with jax.named_scope(f"gather_b{s}"):
            quarter[1][s] = swap(quarter[0][s], ROUNDS[s][1])
    for s in streams:
        with jax.named_scope(f"gather_c{s}"):
            quarter[2][s] = swap(quarter[0][s], ROUNDS[s][2])
        with jax.named_scope(f"gather_d{s}"):
            quarter[3][s] = swap(quarter[1][s], ROUNDS[s][2])

    def step(quarters, added, half, dtypes):
        places = [(q, s) for q in quarters for s in streams]
        return forward(rows, [quarter[q][s] for q, s in places], places, added, half, dtypes)

    with jax.named_scope("forward0"):
        part = step((0, 1), [], None, (F32, F32))
    with jax.named_scope("forward1"):
        own, away = step((2,), part, None, (F32, BF16))
        own_rest = swap_core(away)
    with jax.named_scope("forward2"):
        (away,) = step((3,), [], 1, (BF16,))
        other = swap_core(away)
    with jax.named_scope("forward3"):
        (own,) = step((3,), [own, own_rest], 0, (F32,))
    with jax.named_scope("grad"):
        grad = [joined_grad_of(first, row_counts, own, other, target_rows, norm_gain) for first in (0, row_total // 2)]
        grads = jnp.concatenate(grad + [swap_core(part) for part in grad], 0)

    def product(s, q):
        return jnp.dot(features[s, q * 256 : (q + 1) * 256], grads, preferred_element_type=F32)

    got, kept = [[None] * 3 for _ in range(4)], []
    for s in streams:
        with jax.named_scope(f"reduce_d{s}"):
            got[3][s] = swap(product(s, 3).astype(BF16), ROUNDS[s][2])
    for s in streams:
        with jax.named_scope(f"reduce_c{s}"):
            got[2][s] = swap(product(s, 2).astype(BF16), ROUNDS[s][2])
    for s in streams:
        with jax.named_scope(f"reduce_b{s}"):
            got[1][s] = swap((product(s, 1) + got[3][s].astype(F32)).astype(BF16), ROUNDS[s][1])
    for s in streams:
        with jax.named_scope(f"reduce_a{s}"):
            part = product(s, 0) + got[2][s].astype(F32) + got[1][s].astype(F32)
            got[0][s] = swap(part[128:].astype(BF16), ROUNDS[s][0])
            kept.append((part[:128] + got[0][s].astype(F32)).astype(BF16))
    near = jnp.concatenate(kept, 0)
    owned_grad = jnp.sum(cube_exchange(near).reshape(8, 48, width).astype(F32), axis=0)
    return normalize_rows(owned_grad).astype(BF16)


def solution(mesh):
    return jax.shard_map(
        local,
        mesh=mesh,
        in_specs=(
            P(("replica", "shard"), None),
            P(("replica", "shard")),
            P(("replica", "shard"), None),
            P(("replica", "shard"), None),
            P(),
        ),
        out_specs=P(("replica", "shard"), None),
        check_vma=False,
    )
```
